256 devices in a mesh: ctx: 32 (over z, y_hi, core), tp: 8 (over y_lo, x).
Axes of the slice: x: 4, y: 4 (y_hi: 2, y_lo: 2; y = y_hi * 2 + y_lo), z: 8, core: 2. Of those that a mesh axis runs over, the one named last changes fastest.
Arguments:
- queries: bfloat16 [16384, 8192], P('ctx', 'tp'), may hold values from -132 to 132
- keys: bfloat16 [16384, 1024], P('ctx', 'tp'), may hold values from -6 to 6
- values: bfloat16 [16384, 1024], P('ctx', 'tp'), may hold values from -6 to 6
- prefix_spans: int32 [32], P('ctx'), may hold values from 1 to 7, as said below
Outputs:
- attended: bfloat16 [16384, 8192], P('ctx', 'tp')
The draws below stay inside these ranges and needn't reach their ends.
Inputs may be any that keep to these rules, and one draw needn't show every extreme that they name: `prefix_spans`: 7 is reached by some block in every draw.
All inputs are finite; a program needn't handle non-finite values.
Results may differ from the reference program's by a relative error of at most 0.003.
Values may be sent and summed in bfloat16 or wider, within the bound.
A program may use at most 128 MiB of HBM per device.

```python
import math
import jax
import jax.numpy as jnp
from jax import lax

QUERY_HEAD_COUNT = 64
KEY_VALUE_HEADS = 8
HEAD_SIZE = 128
BLOCK_LENGTH = 512
PREFIX_BLOCK_MAX = 7
TOKEN_COUNT = 16384


def common_pattern(key):
    key_seed_base = jax.random.fold_in(key, 102)
    random_base_keys = jnp.clip(jax.random.normal(key_seed_base, (TOKEN_COUNT, KEY_VALUE_HEADS, HEAD_SIZE), jnp.float32), -6.0, 6.0)
    return random_base_keys


def draw_keys(key, part):
    random_base_keys = common_pattern(key)
    result_output = random_base_keys
    return result_output.reshape(TOKEN_COUNT, KEY_VALUE_HEADS * HEAD_SIZE).astype(jnp.bfloat16)


def draw_queries(key, part):
    key = jax.random.fold_in(key, 2)
    query_group = QUERY_HEAD_COUNT // KEY_VALUE_HEADS
    result_output = jnp.clip(2.5 * jax.random.normal(key, (TOKEN_COUNT, KEY_VALUE_HEADS, query_group, HEAD_SIZE), jnp.float32), -20.0, 20.0)
    return result_output.reshape(TOKEN_COUNT, QUERY_HEAD_COUNT * HEAD_SIZE).astype(jnp.bfloat16)


def draw_prefix_spans(key, part):
    key = jax.random.fold_in(key, 3)
    block_list = TOKEN_COUNT // BLOCK_LENGTH
    counts = jax.random.randint(key, (block_list,), 1, PREFIX_BLOCK_MAX + 1, jnp.int32)
    pick = jax.random.randint(jax.random.fold_in(key, 4), (), 0, block_list, jnp.int32)
    return counts.at[pick].set(PREFIX_BLOCK_MAX)


def level_of(key, extent, shards, low, high):
    gain = 1.0
    for axis_at, blocks in shards:
        steps = jax.random.uniform(jax.random.fold_in(jax.random.fold_in(key, 6), axis_at), (blocks,), jnp.float32, low / len(shards), high / len(shards))
        gain = gain * jnp.repeat(jnp.exp(steps), extent[axis_at] // blocks).reshape((-1,) + (1,) * (len(extent) - 1 - axis_at))
    return gain


def normal_values(own_key, shape, scale, most, pieces=(), kind=jnp.bfloat16):
    drawn = jax.random.normal(own_key, shape, jnp.float32) * scale
    if len(pieces) > 0:
        drawn = level_of(own_key, shape, pieces, -0.22, 0.18) * drawn
    return jnp.clip(drawn, min=-most, max=most).astype(kind)


def setup_inputs(seed: int = 0) -> dict:
    arg_keys = jax.random.split(jax.random.key(seed), 5)
    return {
        "queries": draw_queries(jax.random.fold_in(arg_keys[4], 71), 0),
        "keys": draw_keys(jax.random.fold_in(arg_keys[4], 71), 0),
        "values": normal_values(arg_keys[2], (TOKEN_COUNT, KEY_VALUE_HEADS * HEAD_SIZE), 1.0, 6.0, ((0, 32), (1, 8))),
        "prefix_spans": draw_prefix_spans(jax.random.fold_in(arg_keys[4], 71), 0),
    }


def block_update(running_state, scores, vals):
    running_max, total, acc = running_state
    new_max = jnp.maximum(running_max, lax.optimization_barrier(jnp.max(scores, axis=-1)))
    correct = jnp.exp(running_max - new_max)
    probs = jnp.exp(scores - new_max[..., None])
    total = total * correct + lax.optimization_barrier(jnp.sum(probs, axis=-1))
    rounded = lax.optimization_barrier(probs.astype(jnp.bfloat16))
    acc = acc * correct[..., None] + jnp.einsum('rhgt,thd->rhgd', rounded.astype(jnp.float32), vals)
    return (new_max, total, acc)

def reference(queries, keys, values, prefix_spans):
    query_group = QUERY_HEAD_COUNT // KEY_VALUE_HEADS
    block_list = TOKEN_COUNT // BLOCK_LENGTH
    scale = 1.0 / math.sqrt(HEAD_SIZE)
    query_head_rows = queries.reshape(block_list, BLOCK_LENGTH, KEY_VALUE_HEADS, query_group, HEAD_SIZE)
    key_head_rows = keys.reshape(block_list, BLOCK_LENGTH, KEY_VALUE_HEADS, HEAD_SIZE)
    value_head_rows = values.reshape(block_list, BLOCK_LENGTH, KEY_VALUE_HEADS, HEAD_SIZE)
    padding_width = jnp.zeros((PREFIX_BLOCK_MAX, BLOCK_LENGTH, KEY_VALUE_HEADS, HEAD_SIZE), jnp.bfloat16)
    key_padded = jnp.concatenate([padding_width, key_head_rows], axis=0)
    value_padded = jnp.concatenate([padding_width, value_head_rows], axis=0)
    row_ids = jnp.arange(BLOCK_LENGTH, dtype=jnp.int32)[:, None, None, None]
    col_ids = jnp.arange(BLOCK_LENGTH, dtype=jnp.int32)[None, None, None, :]

    def one_block(index):
        qf = lax.dynamic_index_in_dim(query_head_rows, index, 0, keepdims=False).astype(jnp.float32)
        limit = lax.dynamic_index_in_dim(prefix_spans, index, 0, keepdims=False)
        running_state = (jnp.full((BLOCK_LENGTH, KEY_VALUE_HEADS, query_group), -jnp.inf, jnp.float32), jnp.zeros((BLOCK_LENGTH, KEY_VALUE_HEADS, query_group), jnp.float32), jnp.zeros((BLOCK_LENGTH, KEY_VALUE_HEADS, query_group, HEAD_SIZE), jnp.float32))
        for step in range(PREFIX_BLOCK_MAX + 1):
            where_at = (index + PREFIX_BLOCK_MAX - step).astype(jnp.int32)
            key_block = lax.dynamic_index_in_dim(key_padded, where_at, 0, keepdims=False).astype(jnp.float32)
            value_block = lax.dynamic_index_in_dim(value_padded, where_at, 0, keepdims=False).astype(jnp.float32)
            scores = jnp.einsum('rhgd,thd->rhgt', qf, key_block) * scale
            if step == 0:
                admitted = row_ids >= col_ids
            else:
                admitted = jnp.logical_and(step <= limit, index - step >= 0)
            scores = jnp.where(admitted, scores, -jnp.inf)
            running_state = block_update(running_state, scores, value_block)
        output = running_state[2] / running_state[1][..., None]
        return output.reshape(BLOCK_LENGTH, QUERY_HEAD_COUNT * HEAD_SIZE).astype(jnp.bfloat16)
    result_output = lax.map(one_block, jnp.arange(block_list, dtype=jnp.int32))
    return result_output.reshape(TOKEN_COUNT, QUERY_HEAD_COUNT * HEAD_SIZE)
```

```python
import functools
import math

import jax
import jax.numpy as jnp
from jax import lax
from jax.experimental import pallas as pl
from jax.experimental.pallas import tpu as pltpu
from jax.sharding import PartitionSpec as P

HEAD = 128
HEADS = 8
ROWS = 512
TILE = 256
UNROLL = 8
SCALE = math.log2(math.e) / math.sqrt(HEAD)
HUGE = 3.0e38
MESH = pl.DeviceIdType.MESH
F32 = jnp.float32
BF16 = jnp.bfloat16

OWN, NEAR, SWAP, SIDE, FAR, O_NEAR, O_SWAP, O_SIDE, EXTRA = range(9)
UP, ACROSS, SWAPPED, UP_TWO, ACROSS_TWO, S_NEAR, S_SWAP, S_SIDE, S_EXTRA = range(9)


def kernel(
    z_count, q_ref, k_ref, v_ref, span_ref, o_ref, kt, vb, *rest
):
    accs, maxes = rest[:UNROLL], rest[UNROLL : 2 * UNROLL]
    send_sem, recv_sem = rest[2 * UNROLL :]
    ctx = lax.axis_index("ctx")
    tp = lax.axis_index("tp")
    core = lax.rem(ctx, 2)
    column = lax.rem(ctx // 2, 2)
    z = ctx // 4
    has_down = z > 0
    has_up = z < z_count - 1
    up = (jnp.minimum(ctx + 4, 4 * z_count - 1), tp)
    down = (jnp.maximum(ctx - 4, 0), tp)
    across = (ctx + 2 - 4 * column, tp)
    sibling = (ctx + 1 - 2 * core, tp)

    barrier = pltpu.get_barrier_semaphore()
    pl.semaphore_signal(barrier, inc=1, device_id=across, device_id_type=MESH)
    pl.semaphore_signal(barrier, inc=1, device_id=sibling, device_id_type=MESH)

    @pl.when(has_down)
    def _():
        pl.semaphore_signal(barrier, inc=1, device_id=down, device_id_type=MESH)

    @pl.when(has_up)
    def _():
        pl.semaphore_signal(barrier, inc=1, device_id=up, device_id_type=MESH)

    kt[OWN] = k_ref[...].T
    vb[OWN] = v_ref[...]
    pl.semaphore_wait(barrier, 2 + has_down.astype(jnp.int32) + has_up.astype(jnp.int32))

    def copies(flow, source, target, device):
        return [
            pltpu.make_async_remote_copy(
                src_ref=ref.at[source],
                dst_ref=ref.at[target],
                send_sem=send_sem.at[flow, n],
                recv_sem=recv_sem.at[flow, n],
                device_id=device,
                device_id_type=MESH,
            )
            for n, ref in enumerate((kt, vb))
        ]

    go_up = copies(UP, OWN, NEAR, up)
    go_across = copies(ACROSS, OWN, SIDE, across)
    go_swapped = copies(SWAPPED, NEAR, SWAP, across)
    go_up_two = copies(UP_TWO, NEAR, FAR, up)
    go_across_two = copies(ACROSS_TWO, FAR, SIDE, across)
    go_near = copies(S_NEAR, NEAR, O_NEAR, sibling)
    go_swap = copies(S_SWAP, SWAP, O_SWAP, sibling)
    go_side = copies(S_SIDE, SIDE, O_SIDE, sibling)
    own_to_sibling = copies(S_EXTRA, OWN, EXTRA, sibling)
    far_to_sibling = copies(S_EXTRA, FAR, EXTRA, sibling)

    sends_up_two = has_down & has_up & ((column == 1) | (core == 1))
    gets_far = (z >= 2) & ((column == 1) | (core == 1))
    sends_across_two = (z >= 2) & (column == 1)
    gets_side_two = (z >= 2) & (column == 0)
    gets_side = (column == 1) | (z >= 2)

    @pl.when(core == 0)
    def _():
        for copy in own_to_sibling:
            copy.start()

    for n in range(2):

        @pl.when(has_up)
        def _():
            go_up[n].start()

        @pl.when(column == 0)
        def _():
            go_across[n].start()

    limit = span_ref[0]
    ones = jnp.ones((ROWS, HEAD), BF16)

    def weigh(scores, top):
        pieces = [
            jnp.exp2(scores[:, c : c + HEAD] * SCALE - top).astype(BF16)
            for c in range(0, scores.shape[1], HEAD)
        ]
        return jnp.concatenate(pieces, axis=1)

    def lanes_max(scores):
        best = scores[:, :HEAD]
        for c in range(HEAD, scores.shape[1], HEAD):
            best = jnp.maximum(best, scores[:, c : c + HEAD])
        return best

    def queries(tile):
        head, part = tile // (ROWS // TILE), lax.rem(tile, ROWS // TILE)
        return q_ref[
            pl.ds(pl.multiple_of(part * TILE, TILE), TILE),
            pl.ds(pl.multiple_of(head * HEAD, HEAD), HEAD),
        ]

    def with_ones(block, upto=ROWS):
        return jnp.concatenate([vb[block, :upto], ones[:upto]], axis=1)

    steps = HEADS * ROWS // TILE // UNROLL

    def own_block():
        rows = lax.broadcasted_iota(jnp.int32, (TILE, TILE), 0)
        cols = lax.broadcasted_iota(jnp.int32, (TILE, TILE), 1)

        @pl.loop(0, steps)
        def _(step):
            place = pl.ds(pl.multiple_of(step * TILE, TILE), TILE)
            for u in range(UNROLL):
                part = u % (ROWS // TILE)
                q = queries(step * UNROLL + u)
                upto = (part + 1) * TILE
                scores = jnp.dot(q, kt[OWN, :, :upto], preferred_element_type=F32)
                last = jnp.where(rows >= cols, scores[:, upto - TILE :], -jnp.inf)
                if part:
                    scores = jnp.concatenate([scores[:, : upto - TILE], last], axis=1)
                else:
                    scores = last
                top = jnp.max(lanes_max(scores), axis=1, keepdims=True) * SCALE
                top = jnp.broadcast_to(top, (TILE, HEAD))
                accs[u][place, :] = jnp.dot(
                    weigh(scores, top), with_ones(OWN, upto), preferred_element_type=F32
                )
                maxes[u][place, :] = top

    def attend(blocks):
        admitted = [j <= limit for _, j in blocks]

        @pl.loop(0, steps)
        def _(step):
            place = pl.ds(pl.multiple_of(step * TILE, TILE), TILE)
            for u in range(UNROLL):
                q = queries(step * UNROLL + u)
                before = maxes[u][place, :]
                all_scores = [
                    jnp.dot(q, kt[block], preferred_element_type=F32) for block, _ in blocks
                ]
                best = None
                for scores, fits in zip(all_scores, admitted):
                    mine = jnp.where(fits, lanes_max(scores), -jnp.inf)
                    best = mine if best is None else jnp.maximum(best, mine)
                best = jnp.max(best, axis=1, keepdims=True) * SCALE
                top = jnp.maximum(before, best)
                correct = jnp.exp2(before - top)
                acc = accs[u][place, :] * jnp.concatenate([correct, correct], axis=1)
                for (block, _), scores, fits in zip(blocks, all_scores, admitted):
                    acc += jnp.dot(
                        weigh(scores, jnp.where(fits, top, HUGE)),
                        with_ones(block),
                        preferred_element_type=F32,
                    )
                accs[u][place, :] = acc
                maxes[u][place, :] = top

    def wait_recv(flow):
        for copy in flow:
            copy.wait_recv()

    def pass_on(*flows):
        for pair in zip(*flows):
            for copy in pair:
                copy.start()

    def distance(chips):
        return 2 * chips, 2 * chips - 1 + 2 * core

    own_block()

    for n in range(2):

        @pl.when(has_down)
        def _():
            go_up[n].wait_recv()
            go_swapped[n].start()
            go_near[n].start()

        @pl.when(sends_up_two)
        def _():
            go_up_two[n].start()

    @pl.when(column == 1)
    def _():
        wait_recv(go_across)
        pass_on(go_side)

    @pl.when(core == 1)
    def _():
        wait_recv(own_to_sibling)
        attend([(EXTRA, 1)])

    @pl.when(has_down)
    def _():
        wait_recv(go_near)
        mine, other = distance(2)
        attend([(NEAR, mine), (O_NEAR, other)])

    @pl.when(gets_far)
    def _():
        wait_recv(go_up_two)

    @pl.when(sends_across_two)
    def _():
        pass_on(go_across_two)

    @pl.when((z >= 2) & (core == 1))
    def _():
        pass_on(far_to_sibling)

    @pl.when(has_down)
    def _():
        wait_recv(go_swapped)
        pass_on(go_swap)
        wait_recv(go_swap)
        mine, other = distance(1 + 2 * column)
        attend([(SWAP, mine), (O_SWAP, other)])

    @pl.when(gets_side_two)
    def _():
        wait_recv(go_across_two)
        pass_on(go_side)

    @pl.when((z >= 2) & (core == 0))
    def _():
        wait_recv(far_to_sibling)
        attend([(EXTRA, 7)])

    @pl.when(gets_side)
    def _():
        wait_recv(go_side)
        mine, other = distance(3 - 2 * column)
        attend([(SIDE, mine), (O_SIDE, other)])

    for step in range(steps):
        for u in range(UNROLL):
            tile = step * UNROLL + u
            head, part = divmod(tile, ROWS // TILE)
            acc = accs[u][step * TILE : (step + 1) * TILE, :]
            o_ref[part * TILE : (part + 1) * TILE, head * HEAD : (head + 1) * HEAD] = (
                acc[:, :HEAD] / acc[:, HEAD:]
            ).astype(BF16)

    for when, flow in (
        (has_up, go_up),
        (column == 0, go_across),
        (has_down, go_swapped),
        (sends_up_two, go_up_two),
        (sends_across_two, go_across_two),
        (has_down, go_near),
        (has_down, go_swap),
        (gets_side, go_side),
        (core == 0, own_to_sibling),
        ((z >= 2) & (core == 1), far_to_sibling),
    ):

        @pl.when(when)
        def _(flow=flow):
            for copy in flow:
                copy.wait_send()


def on_device(z_count, queries, keys, values, spans):
    vmem = pl.BlockSpec(memory_space=pltpu.VMEM)
    per_tile = HEADS * ROWS // UNROLL
    return pl.pallas_call(
        functools.partial(kernel, z_count),
        out_shape=jax.ShapeDtypeStruct(queries.shape, BF16),
        in_specs=[vmem, vmem, vmem, pl.BlockSpec(memory_space=pltpu.SMEM)],
        out_specs=vmem,
        scratch_shapes=[
            pltpu.VMEM((9, HEAD, ROWS), BF16),
            pltpu.VMEM((9, ROWS, HEAD), BF16),
        ]
        + [pltpu.VMEM((per_tile, 2 * HEAD), F32)] * UNROLL
        + [pltpu.VMEM((per_tile, HEAD), F32)] * UNROLL
        + [pltpu.SemaphoreType.DMA((9, 2)), pltpu.SemaphoreType.DMA((9, 2))],
        compiler_params=pltpu.CompilerParams(
            collective_id=1, has_side_effects=True, vmem_limit_bytes=56 * 2**20
        ),
    )(queries, keys, values, spans)


def solution(mesh):
    placed = (P("ctx", "tp"), P("ctx", "tp"), P("ctx", "tp"), P("ctx"))
    return jax.shard_map(
        functools.partial(on_device, mesh.shape["ctx"] // 4),
        mesh=mesh,
        in_specs=placed,
        out_specs=P("ctx", "tp"),
        check_vma=False,
    )
```

```python
import functools
import math

import jax
import jax.numpy as jnp
from jax import lax
from jax.experimental import pallas as pl
from jax.experimental.pallas import tpu as pltpu
from jax.sharding import PartitionSpec as P

HEAD = 128
HEADS = 8
ROWS = 512
TILE = 256
TILES = HEADS * ROWS // TILE
SCALE = math.log2(math.e) / math.sqrt(HEAD)
HUGE = 3.0e38
MESH = pl.DeviceIdType.MESH
F32 = jnp.float32
BF16 = jnp.bfloat16

OWN, ONE, TWO, THREE, FAR, O_ONE, O_TWO, O_THREE, EXTRA = range(9)
UP, ACROSS, SWAPPED, UP_TWO, ACROSS_FAR, UP_ONE, S_ONE, S_TWO, S_THREE, S_EXTRA = range(10)


def kernel(
    z_count, q_hbm, k_hbm, v_hbm, span_ref, o_ref, q_ref, k_ref, kt, vb, acc_ref, max_ref,
    send_sem, recv_sem, load_sem
):
    ctx = lax.axis_index("ctx")
    tp = lax.axis_index("tp")
    core = lax.rem(ctx, 2)
    column = lax.rem(ctx // 2, 2)
    z = ctx // 4
    has_down = z > 0
    has_up = z < z_count - 1
    up = (jnp.minimum(ctx + 4, 4 * z_count - 1), tp)
    down = (jnp.maximum(ctx - 4, 0), tp)
    across = (ctx + 2 - 4 * column, tp)
    sibling = (ctx + 1 - 2 * core, tp)

    loads = [
        pltpu.make_async_copy(source, target, load_sem.at[n])
        for n, (source, target) in enumerate(
            ((k_hbm, k_ref), (v_hbm, vb.at[OWN]), (q_hbm, q_ref))
        )
    ]
    for load in loads:
        load.start()

    barrier = pltpu.get_barrier_semaphore()

    pl.semaphore_signal(barrier, inc=1, device_id=across, device_id_type=MESH)
    pl.semaphore_signal(barrier, inc=1, device_id=sibling, device_id_type=MESH)

    @pl.when(has_down)
    def _():
        pl.semaphore_signal(barrier, inc=1, device_id=down, device_id_type=MESH)

    @pl.when(has_up)
    def _():
        pl.semaphore_signal(barrier, inc=1, device_id=up, device_id_type=MESH)

    loads[0].wait()
    kt[OWN] = k_ref[...].T
    loads[1].wait()
    loads[2].wait()

    def copies(flow, source, target, device):
        return [
            pltpu.make_async_remote_copy(
                src_ref=ref.at[source],
                dst_ref=ref.at[target],
                send_sem=send_sem.at[flow, n],
                recv_sem=recv_sem.at[flow, n],
                device_id=device,
                device_id_type=MESH,
            )
            for n, ref in enumerate((kt, vb))
        ]

    go_up = copies(UP, OWN, TWO, up)
    go_across = copies(ACROSS, OWN, ONE, across)
    go_swapped = copies(SWAPPED, TWO, jnp.where(column == 0, THREE, ONE), across)
    go_up_two = copies(UP_TWO, TWO, FAR, up)
    go_across_far = copies(ACROSS_FAR, FAR, THREE, across)
    go_up_one = copies(UP_ONE, ONE, THREE, up)
    go_one = copies(S_ONE, ONE, O_ONE, sibling)
    go_two = copies(S_TWO, TWO, O_TWO, sibling)
    go_three = copies(S_THREE, THREE, O_THREE, sibling)
    own_to_sibling = copies(S_EXTRA, OWN, EXTRA, sibling)
    far_to_sibling = copies(S_EXTRA, FAR, EXTRA, sibling)

    has_far = z >= 2
    sends_up_two = has_down & has_up & (core == 1)
    sends_across_far = has_far & (column == 1) & (core == 1)
    sends_up_one = has_down & has_up & (column == 0) & (core == 0)
    has_one = (column == 1) | has_down
    has_three = jnp.where(column == 1, has_down, has_far)

    limit = span_ref[0]
    ones = jnp.ones((ROWS, HEAD), BF16)

    def weigh(scores, top):
        pieces = [
            jnp.exp2(scores[:, c : c + HEAD] * SCALE - top).astype(BF16)
            for c in range(0, scores.shape[1], HEAD)
        ]
        return jnp.concatenate(pieces, axis=1)

    def lanes_max(scores):
        best = scores[:, :HEAD]
        for c in range(HEAD, scores.shape[1], HEAD):
            best = jnp.maximum(best, scores[:, c : c + HEAD])
        return best

    def queries(tile):
        head, part = divmod(tile, ROWS // TILE)
        return q_ref[part * TILE : (part + 1) * TILE, head * HEAD : (head + 1) * HEAD]

    def finish(tile, acc):
        head, part = divmod(tile, ROWS // TILE)
        o_ref[part * TILE : (part + 1) * TILE, head * HEAD : (head + 1) * HEAD] = (
            acc[:, :HEAD] / acc[:, HEAD:]
        ).astype(BF16)

    def with_ones(block, upto=ROWS):
        return jnp.concatenate([vb[block, :upto], ones[:upto]], axis=1)

    def own_block(tiles):
        rows = lax.broadcasted_iota(jnp.int32, (TILE, TILE), 0)
        cols = lax.broadcasted_iota(jnp.int32, (TILE, TILE), 1)
        for tile in tiles:
            part = tile % (ROWS // TILE)
            upto = (part + 1) * TILE
            scores = jnp.dot(queries(tile), kt[OWN, :, :upto], preferred_element_type=F32)
            last = jnp.where(rows >= cols, scores[:, upto - TILE :], -jnp.inf)
            if part:
                scores = jnp.concatenate([scores[:, : upto - TILE], last], axis=1)
            else:
                scores = last
            top = jnp.max(lanes_max(scores), axis=1, keepdims=True) * SCALE
            top = jnp.broadcast_to(top, (TILE, HEAD))
            acc_ref[tile] = jnp.dot(
                weigh(scores, top), with_ones(OWN, upto), preferred_element_type=F32
            )
            max_ref[tile] = top

    def attend(blocks, last=False):
        admitted = [j <= limit for _, j in blocks]
        for tile in range(TILES):
            q = queries(tile)
            before = max_ref[tile]
            all_scores = [
                jnp.dot(q, kt[block], preferred_element_type=F32) for block, _ in blocks
            ]
            best = None
            for scores, fits in zip(all_scores, admitted):
                mine = jnp.where(fits, lanes_max(scores), -jnp.inf)
                best = mine if best is None else jnp.maximum(best, mine)
            best = jnp.max(best, axis=1, keepdims=True) * SCALE
            top = jnp.maximum(before, best)
            correct = jnp.exp2(before - top)
            acc = acc_ref[tile] * jnp.concatenate([correct, correct], axis=1)
            for (block, _), scores, fits in zip(blocks, all_scores, admitted):
                acc += jnp.dot(
                    weigh(scores, jnp.where(fits, top, HUGE)),
                    with_ones(block),
                    preferred_element_type=F32,
                )
            if last:
                finish(tile, acc)
            else:
                acc_ref[tile] = acc
                max_ref[tile] = top

    def wait_recv(flow):
        for copy in flow:
            copy.wait_recv()

    def pass_on(*flows):
        for pair in zip(*flows):
            for copy in pair:
                copy.start()

    def distance(chips):
        return 2 * chips, 2 * chips - 1 + 2 * core

    own_block(range(TILES // 2))
    pl.semaphore_wait(
        barrier, 2 + sum(some.astype(jnp.int32) for some in (has_down, has_up))
    )

    @pl.when(core == 0)
    def _():
        for copy in own_to_sibling:
            copy.start()

    for n in range(2):

        @pl.when(has_up)
        def _():
            go_up[n].start()

        @pl.when(column == 0)
        def _():
            go_across[n].start()

    own_block(range(TILES // 2, TILES))

    @pl.when(core == 1)
    def _():
        wait_recv(own_to_sibling)
        attend([(EXTRA, 1)])

    for n in range(2):

        @pl.when(has_down)
        def _():
            go_up[n].wait_recv()
            go_two[n].start()
            go_swapped[n].start()

        @pl.when(sends_up_two)
        def _():
            go_up_two[n].start()

    @pl.when(column == 1)
    def _():
        wait_recv(go_across)
        pass_on(go_one)

    @pl.when(has_down)
    def _():
        wait_recv(go_two)
        mine, other = distance(2)
        attend([(TWO, mine), (O_TWO, other)])
        wait_recv(go_swapped)

    @pl.when(has_down & (column == 0))
    def _():
        pass_on(go_one)

    @pl.when(sends_up_one)
    def _():
        pass_on(go_up_one)

    @pl.when(has_far & (core == 1))
    def _():
        wait_recv(go_up_two)

    @pl.when(sends_across_far)
    def _():
        pass_on(go_across_far)

    @pl.when(has_far & (core == 1))
    def _():
        pass_on(far_to_sibling)

    @pl.when(has_down & (column == 1))
    def _():
        pass_on(go_three)

    @pl.when(has_one)
    def _():
        wait_recv(go_one)
        mine, other = distance(1)
        attend([(ONE, mine), (O_ONE, other)])

    @pl.when(has_far & (column == 0) & (core == 0))
    def _():
        wait_recv(go_up_one)

    @pl.when(has_far & (column == 0) & (core == 1))
    def _():
        wait_recv(go_across_far)

    @pl.when(has_far & (column == 0))
    def _():
        pass_on(go_three)

    @pl.when(has_far & (core == 0))
    def _():
        wait_recv(far_to_sibling)
        attend([(EXTRA, 7)])

    @pl.when(has_three)
    def _():
        wait_recv(go_three)
        mine, other = distance(3)
        attend([(THREE, mine), (O_THREE, other)], last=True)

    @pl.when(jnp.logical_not(has_three))
    def _():
        for tile in range(TILES):
            finish(tile, acc_ref[tile])

    for when, flow in (
        (has_up, go_up),
        (column == 0, go_across),
        (has_down, go_swapped),
        (sends_up_two, go_up_two),
        (sends_across_far, go_across_far),
        (sends_up_one, go_up_one),
        (has_one, go_one),
        (has_down, go_two),
        (has_three, go_three),
        (core == 0, own_to_sibling),
        (has_far & (core == 1), far_to_sibling),
    ):

        @pl.when(when)
        def _(flow=flow):
            for copy in flow:
                copy.wait_send()


def on_device(z_count, queries, keys, values, spans):
    shape = jax.ShapeDtypeStruct(queries.shape, BF16)
    return pl.pallas_call(
        functools.partial(kernel, z_count),
        out_shape=shape,
        in_specs=[pl.BlockSpec(memory_space=pltpu.HBM)] * 3 + [pl.BlockSpec(memory_space=pltpu.SMEM)],
        out_specs=pl.BlockSpec(memory_space=pltpu.VMEM),
        scratch_shapes=[
            pltpu.VMEM(queries.shape, BF16),
            pltpu.VMEM(keys.shape, BF16),
            pltpu.VMEM((9, HEAD, ROWS), BF16),
            pltpu.VMEM((9, ROWS, HEAD), BF16),
            pltpu.VMEM((TILES, TILE, 2 * HEAD), F32),
            pltpu.VMEM((TILES, TILE, HEAD), F32),
            pltpu.SemaphoreType.DMA((10, 2)),
            pltpu.SemaphoreType.DMA((10, 2)),
            pltpu.SemaphoreType.DMA((3,)),
        ],
        compiler_params=pltpu.CompilerParams(
            collective_id=1, has_side_effects=True, vmem_limit_bytes=52 * 2**20
        ),
    )(queries, keys, values, spans)


def solution(mesh):
    placed = (P("ctx", "tp"), P("ctx", "tp"), P("ctx", "tp"), P("ctx"))
    return jax.shard_map(
        functools.partial(on_device, mesh.shape["ctx"] // 4),
        mesh=mesh,
        in_specs=placed,
        out_specs=P("ctx", "tp"),
        check_vma=False,
    )
```

```python
import functools
import math

import jax
import jax.numpy as jnp
from jax import lax
from jax.experimental import pallas as pl
from jax.experimental.pallas import tpu as pltpu
from jax.sharding import PartitionSpec as P

HEAD = 128
HEADS = 8
ROWS = 512
TILE = 256
TILES = HEADS * ROWS // TILE
SCALE = math.log2(math.e) / math.sqrt(HEAD)
HUGE = 3.0e38
MESH = pl.DeviceIdType.MESH
F32 = jnp.float32
BF16 = jnp.bfloat16

OWN, ONE, TWO, THREE, FAR, O_ONE, O_TWO, O_THREE, EXTRA = range(9)
UP, ACROSS, SWAPPED, UP_TWO, ACROSS_FAR, UP_ONE, S_ONE, S_TWO, S_THREE, S_EXTRA = range(10)


def kernel(
    z_count, q_hbm, k_hbm, v_hbm, span_ref, o_ref, q_ref, k_ref, kt, vb, acc_ref, max_ref,
    send_sem, recv_sem, load_sem
):
    ctx = lax.axis_index("ctx")
    tp = lax.axis_index("tp")
    core = lax.rem(ctx, 2)
    column = lax.rem(ctx // 2, 2)
    z = ctx // 4
    has_down = z > 0
    has_up = z < z_count - 1
    up = (jnp.minimum(ctx + 4, 4 * z_count - 1), tp)
    down = (jnp.maximum(ctx - 4, 0), tp)
    across = (ctx + 2 - 4 * column, tp)
    sibling = (ctx + 1 - 2 * core, tp)

    loads = [
        pltpu.make_async_copy(source, target, load_sem.at[n])
        for n, (source, target) in enumerate(
            ((k_hbm, k_ref), (v_hbm, vb.at[OWN]), (q_hbm, q_ref))
        )
    ]
    for load in loads:
        load.start()

    barrier = pltpu.get_barrier_semaphore()

    pl.semaphore_signal(barrier, inc=1, device_id=across, device_id_type=MESH)
    pl.semaphore_signal(barrier, inc=1, device_id=sibling, device_id_type=MESH)

    @pl.when(has_down)
    def _():
        pl.semaphore_signal(barrier, inc=1, device_id=down, device_id_type=MESH)

    @pl.when(has_up)
    def _():
        pl.semaphore_signal(barrier, inc=1, device_id=up, device_id_type=MESH)

    loads[0].wait()
    kt[OWN] = k_ref[...].T
    loads[1].wait()
    loads[2].wait()

    def copies(flow, source, target, device):
        return [
            pltpu.make_async_remote_copy(
                src_ref=ref.at[source],
                dst_ref=ref.at[target],
                send_sem=send_sem.at[flow, n],
                recv_sem=recv_sem.at[flow, n],
                device_id=device,
                device_id_type=MESH,
            )
            for n, ref in enumerate((kt, vb))
        ]

    go_up = copies(UP, OWN, TWO, up)
    go_across = copies(ACROSS, OWN, ONE, across)
    go_swapped = copies(SWAPPED, TWO, jnp.where(column == 0, THREE, ONE), across)
    go_up_two = copies(UP_TWO, TWO, FAR, up)
    go_across_far = copies(ACROSS_FAR, FAR, THREE, across)
    go_up_one = copies(UP_ONE, ONE, THREE, up)
    go_one = copies(S_ONE, ONE, O_ONE, sibling)
    go_two = copies(S_TWO, TWO, O_TWO, sibling)
    go_three = copies(S_THREE, THREE, O_THREE, sibling)
    own_to_sibling = copies(S_EXTRA, OWN, EXTRA, sibling)
    far_to_sibling = copies(S_EXTRA, FAR, EXTRA, sibling)

    has_far = z >= 2
    sends_up_two = has_down & has_up & (core == 1)
    sends_across_far = has_far & (column == 1) & (core == 1)
    sends_up_one = has_down & has_up & (column == 0) & (core == 0)
    has_one = (column == 1) | has_down
    has_three = jnp.where(column == 1, has_down, has_far)

    limit = span_ref[0]
    ones = jnp.ones((ROWS, HEAD), BF16)

    def weigh(scores, top):
        pieces = [
            jnp.exp2(scores[:, c : c + HEAD] * SCALE - top).astype(BF16)
            for c in range(0, scores.shape[1], HEAD)
        ]
        return jnp.concatenate(pieces, axis=1)

    def lanes_max(scores):
        best = scores[:, :HEAD]
        for c in range(HEAD, scores.shape[1], HEAD):
            best = jnp.maximum(best, scores[:, c : c + HEAD])
        return best

    def queries(tile):
        head, part = divmod(tile, ROWS // TILE)
        return q_ref[part * TILE : (part + 1) * TILE, head * HEAD : (head + 1) * HEAD]

    def finish(tile, acc):
        head, part = divmod(tile, ROWS // TILE)
        o_ref[part * TILE : (part + 1) * TILE, head * HEAD : (head + 1) * HEAD] = (
            acc[:, :HEAD] / acc[:, HEAD:]
        ).astype(BF16)

    def with_ones(block, upto=ROWS):
        return jnp.concatenate([vb[block, :upto], ones[:upto]], axis=1)

    def own_block(tiles):
        rows = lax.broadcasted_iota(jnp.int32, (TILE, TILE), 0)
        cols = lax.broadcasted_iota(jnp.int32, (TILE, TILE), 1)
        for tile in tiles:
            part = tile % (ROWS // TILE)
            upto = (part + 1) * TILE
            scores = jnp.dot(queries(tile), kt[OWN, :, :upto], preferred_element_type=F32)
            last = jnp.where(rows >= cols, scores[:, upto - TILE :], -jnp.inf)
            if part:
                scores = jnp.concatenate([scores[:, : upto - TILE], last], axis=1)
            else:
                scores = last
            top = jnp.max(lanes_max(scores), axis=1, keepdims=True) * SCALE
            top = jnp.broadcast_to(top, (TILE, HEAD))
            acc_ref[tile] = jnp.dot(
                weigh(scores, top), with_ones(OWN, upto), preferred_element_type=F32
            )
            max_ref[tile] = top

    def attend(blocks, last=False):
        admitted = [j <= limit for _, j in blocks]
        for tile in range(TILES):
            q = queries(tile)
            before = max_ref[tile]
            all_scores = [
                jnp.dot(q, kt[block], preferred_element_type=F32) for block, _ in blocks
            ]
            best = None
            for scores, fits in zip(all_scores, admitted):
                mine = jnp.where(fits, lanes_max(scores), -jnp.inf)
                best = mine if best is None else jnp.maximum(best, mine)
            best = jnp.max(best, axis=1, keepdims=True) * SCALE
            top = jnp.maximum(before, best)
            correct = jnp.exp2(before - top)
            acc = acc_ref[tile] * jnp.concatenate([correct, correct], axis=1)
            for (block, _), scores, fits in zip(blocks, all_scores, admitted):
                acc += jnp.dot(
                    weigh(scores, jnp.where(fits, top, HUGE)),
                    with_ones(block),
                    preferred_element_type=F32,
                )
            if last:
                finish(tile, acc)
            else:
                acc_ref[tile] = acc
                max_ref[tile] = top

    def wait_recv(flow):
        for copy in flow:
            copy.wait_recv()

    def pass_on(*flows):
        for pair in zip(*flows):
            for copy in pair:
                copy.start()

    def distance(chips):
        return 2 * chips, 2 * chips - 1 + 2 * core

    own_block(range(TILES // 2))
    pl.semaphore_wait(
        barrier, 2 + sum(some.astype(jnp.int32) for some in (has_down, has_up))
    )

    @pl.when(core == 0)
    def _():
        for copy in own_to_sibling:
            copy.start()

    for n in range(2):

        @pl.when(has_up)
        def _():
            go_up[n].start()

        @pl.when(column == 0)
        def _():
            go_across[n].start()

    own_block(range(TILES // 2, TILES))

    @pl.when(core == 1)
    def _():
        wait_recv(own_to_sibling)
        attend([(EXTRA, 1)])

    for n in range(2):

        @pl.when(has_down)
        def _():
            go_up[n].wait_recv()
            go_two[n].start()
            go_swapped[n].start()

        @pl.when(sends_up_two)
        def _():
            go_up_two[n].start()

    @pl.when(column == 1)
    def _():
        wait_recv(go_across)
        pass_on(go_one)

    @pl.when(has_down)
    def _():
        wait_recv(go_two)
        mine, other = distance(2)
        attend([(TWO, mine), (O_TWO, other)])
        wait_recv(go_swapped)

    @pl.when(has_down & (column == 0))
    def _():
        pass_on(go_one)

    @pl.when(sends_up_one)
    def _():
        pass_on(go_up_one)

    @pl.when(has_far & (core == 1))
    def _():
        wait_recv(go_up_two)

    @pl.when(sends_across_far)
    def _():
        pass_on(go_across_far)

    @pl.when(has_far & (core == 1))
    def _():
        pass_on(far_to_sibling)

    @pl.when(has_down & (column == 1))
    def _():
        pass_on(go_three)

    @pl.when(has_one)
    def _():
        wait_recv(go_one)
        mine, other = distance(1)
        attend([(ONE, mine), (O_ONE, other)])

    @pl.when(has_far & (column == 0) & (core == 0))
    def _():
        wait_recv(go_up_one)

    @pl.when(has_far & (column == 0) & (core == 1))
    def _():
        wait_recv(go_across_far)

    @pl.when(has_far & (column == 0))
    def _():
        pass_on(go_three)

    @pl.when(has_far & (core == 0))
    def _():
        wait_recv(far_to_sibling)
        attend([(EXTRA, 7)])

    @pl.when(has_three)
    def _():
        wait_recv(go_three)
        mine, other = distance(3)
        attend([(THREE, mine), (O_THREE, other)], last=True)

    @pl.when(jnp.logical_not(has_three))
    def _():
        for tile in range(TILES):
            finish(tile, acc_ref[tile])

    for when, flow in (
        (has_up, go_up),
        (column == 0, go_across),
        (has_down, go_swapped),
        (sends_up_two, go_up_two),
        (sends_across_far, go_across_far),
        (sends_up_one, go_up_one),
        (has_one, go_one),
        (has_down, go_two),
        (has_three, go_three),
        (core == 0, own_to_sibling),
        (has_far & (core == 1), far_to_sibling),
    ):

        @pl.when(when)
        def _(flow=flow):
            for copy in flow:
                copy.wait_send()


def on_device(z_count, queries, keys, values, spans):
    shape = jax.ShapeDtypeStruct(queries.shape, BF16)
    queries, keys, values = (
        pltpu.with_memory_space_constraint(array, pltpu.HBM) for array in (queries, keys, values)
    )
    return pl.pallas_call(
        functools.partial(kernel, z_count),
        out_shape=shape,
        in_specs=[pl.BlockSpec(memory_space=pltpu.HBM)] * 3 + [pl.BlockSpec(memory_space=pltpu.SMEM)],
        out_specs=pl.BlockSpec(memory_space=pltpu.VMEM),
        scratch_shapes=[
            pltpu.VMEM(queries.shape, BF16),
            pltpu.VMEM(keys.shape, BF16),
            pltpu.VMEM((9, HEAD, ROWS), BF16),
            pltpu.VMEM((9, ROWS, HEAD), BF16),
            pltpu.VMEM((TILES, TILE, 2 * HEAD), F32),
            pltpu.VMEM((TILES, TILE, HEAD), F32),
            pltpu.SemaphoreType.DMA((10, 2)),
            pltpu.SemaphoreType.DMA((10, 2)),
            pltpu.SemaphoreType.DMA((3,)),
        ],
        compiler_params=pltpu.CompilerParams(
            collective_id=1, has_side_effects=True, vmem_limit_bytes=52 * 2**20
        ),
    )(queries, keys, values, spans)


def solution(mesh):
    placed = (P("ctx", "tp"), P("ctx", "tp"), P("ctx", "tp"), P("ctx"))
    return jax.shard_map(
        functools.partial(on_device, mesh.shape["ctx"] // 4),
        mesh=mesh,
        in_specs=placed,
        out_specs=P("ctx", "tp"),
        check_vma=False,
    )
```

```python
import functools
import math

import jax
import jax.numpy as jnp
from jax import lax
from jax.experimental import pallas as pl
from jax.experimental.pallas import tpu as pltpu
from jax.sharding import PartitionSpec as P

HEAD = 128
HEADS = 8
ROWS = 512
TILE = 256
TILES = HEADS * ROWS // TILE
SCALE = math.log2(math.e) / math.sqrt(HEAD)
HUGE = 3.0e38
MESH = pl.DeviceIdType.MESH
F32 = jnp.float32
BF16 = jnp.bfloat16

OWN, ONE, TWO, THREE, FAR, O_ONE, O_TWO, O_THREE, EXTRA = range(9)
UP, ACROSS, SWAPPED, UP_TWO, ACROSS_FAR, UP_ONE, S_ONE, S_TWO, S_THREE, S_EXTRA = range(10)


def kernel(
    z_count, q_hbm, k_hbm, v_hbm, span_ref, o_ref, q_ref, k_ref, kt, vb, acc_ref, max_ref,
    send_sem, recv_sem, load_sem
):
    ctx = lax.axis_index("ctx")
    tp = lax.axis_index("tp")
    core = lax.rem(ctx, 2)
    column = lax.rem(ctx // 2, 2)
    z = ctx // 4
    has_down = z > 0
    has_up = z < z_count - 1
    up = (jnp.minimum(ctx + 4, 4 * z_count - 1), tp)
    down = (jnp.maximum(ctx - 4, 0), tp)
    across = (ctx + 2 - 4 * column, tp)
    sibling = (ctx + 1 - 2 * core, tp)

    loads = [
        pltpu.make_async_copy(source, target, load_sem.at[n])
        for n, (source, target) in enumerate(
            ((k_hbm, k_ref), (v_hbm, vb.at[OWN]), (q_hbm, q_ref))
        )
    ]
    for load in loads:
        load.start()

    barrier = pltpu.get_barrier_semaphore()

    pl.semaphore_signal(barrier, inc=1, device_id=across, device_id_type=MESH)
    pl.semaphore_signal(barrier, inc=1, device_id=sibling, device_id_type=MESH)

    @pl.when(has_down)
    def _():
        pl.semaphore_signal(barrier, inc=1, device_id=down, device_id_type=MESH)

    @pl.when(has_up)
    def _():
        pl.semaphore_signal(barrier, inc=1, device_id=up, device_id_type=MESH)

    loads[0].wait()
    kt[OWN] = k_ref[...].T
    loads[1].wait()
    loads[2].wait()

    def copies(flow, source, target, device):
        return [
            pltpu.make_async_remote_copy(
                src_ref=ref.at[source],
                dst_ref=ref.at[target],
                send_sem=send_sem.at[flow, n],
                recv_sem=recv_sem.at[flow, n],
                device_id=device,
                device_id_type=MESH,
            )
            for n, ref in enumerate((kt, vb))
        ]

    go_up = copies(UP, OWN, TWO, up)
    go_across = copies(ACROSS, OWN, ONE, across)
    go_swapped = copies(SWAPPED, TWO, jnp.where(column == 0, THREE, ONE), across)
    go_up_two = copies(UP_TWO, TWO, FAR, up)
    go_across_far = copies(ACROSS_FAR, FAR, THREE, across)
    go_up_one = copies(UP_ONE, ONE, THREE, up)
    go_one = copies(S_ONE, ONE, O_ONE, sibling)
    go_two = copies(S_TWO, TWO, O_TWO, sibling)
    go_three = copies(S_THREE, THREE, O_THREE, sibling)
    own_to_sibling = copies(S_EXTRA, OWN, EXTRA, sibling)
    far_to_sibling = copies(S_EXTRA, FAR, EXTRA, sibling)

    has_far = z >= 2
    sends_up_two = has_down & has_up & (core == 1)
    sends_across_far = has_far & (column == 1) & (core == 1)
    sends_up_one = has_down & has_up & (column == 0) & (core == 0)
    has_one = (column == 1) | has_down
    has_three = jnp.where(column == 1, has_down, has_far)

    limit = span_ref[0]
    ones = jnp.ones((ROWS, HEAD), BF16)

    def weigh(scores, top):
        pieces = [
            jnp.exp2(scores[:, c : c + HEAD] * SCALE - top).astype(BF16)
            for c in range(0, scores.shape[1], HEAD)
        ]
        return jnp.concatenate(pieces, axis=1)

    def lanes_max(scores):
        best = scores[:, :HEAD]
        for c in range(HEAD, scores.shape[1], HEAD):
            best = jnp.maximum(best, scores[:, c : c + HEAD])
        return best

    def queries(tile):
        head, part = divmod(tile, ROWS // TILE)
        return q_ref[part * TILE : (part + 1) * TILE, head * HEAD : (head + 1) * HEAD]

    def finish(tile, acc):
        head, part = divmod(tile, ROWS // TILE)
        o_ref[part * TILE : (part + 1) * TILE, head * HEAD : (head + 1) * HEAD] = (
            acc[:, :HEAD] / acc[:, HEAD:]
        ).astype(BF16)

    def with_ones(block, upto=ROWS):
        return jnp.concatenate([vb[block, :upto], ones[:upto]], axis=1)

    def own_block(tiles):
        rows = lax.broadcasted_iota(jnp.int32, (TILE, TILE), 0)
        cols = lax.broadcasted_iota(jnp.int32, (TILE, TILE), 1)
        for tile in tiles:
            part = tile % (ROWS // TILE)
            upto = (part + 1) * TILE
            scores = jnp.dot(queries(tile), kt[OWN, :, :upto], preferred_element_type=F32)
            last = jnp.where(rows >= cols, scores[:, upto - TILE :], -jnp.inf)
            if part:
                scores = jnp.concatenate([scores[:, : upto - TILE], last], axis=1)
            else:
                scores = last
            top = jnp.max(lanes_max(scores), axis=1, keepdims=True) * SCALE
            top = jnp.broadcast_to(top, (TILE, HEAD))
            acc_ref[tile] = jnp.dot(
                weigh(scores, top), with_ones(OWN, upto), preferred_element_type=F32
            )
            max_ref[tile] = top

    def attend(blocks, last=False):
        admitted = [j <= limit for _, j in blocks]
        for tile in range(TILES):
            q = queries(tile)
            before = max_ref[tile]
            all_scores = [
                jnp.dot(q, kt[block], preferred_element_type=F32) for block, _ in blocks
            ]
            best = None
            for scores, fits in zip(all_scores, admitted):
                mine = jnp.where(fits, lanes_max(scores), -jnp.inf)
                best = mine if best is None else jnp.maximum(best, mine)
            best = jnp.max(best, axis=1, keepdims=True) * SCALE
            top = jnp.maximum(before, best)
            correct = jnp.exp2(before - top)
            acc = acc_ref[tile] * jnp.concatenate([correct, correct], axis=1)
            for (block, _), scores, fits in zip(blocks, all_scores, admitted):
                acc += jnp.dot(
                    weigh(scores, jnp.where(fits, top, HUGE)),
                    with_ones(block),
                    preferred_element_type=F32,
                )
            if last:
                finish(tile, acc)
            else:
                acc_ref[tile] = acc
                max_ref[tile] = top

    def wait_recv(flow):
        for copy in flow:
            copy.wait_recv()

    def pass_on(*flows):
        for pair in zip(*flows):
            for copy in pair:
                copy.start()

    def distance(chips):
        return 2 * chips, 2 * chips - 1 + 2 * core

    own_block(range(TILES // 2))
    pl.semaphore_wait(
        barrier, 2 + sum(some.astype(jnp.int32) for some in (has_down, has_up))
    )

    @pl.when(core == 0)
    def _():
        for copy in own_to_sibling:
            copy.start()

    for n in range(2):

        @pl.when(has_up)
        def _():
            go_up[n].start()

        @pl.when(column == 0)
        def _():
            go_across[n].start()

    own_block(range(TILES // 2, TILES))

    @pl.when(core == 1)
    def _():
        wait_recv(own_to_sibling)
        attend([(EXTRA, 1)])

    for n in range(2):

        @pl.when(has_down)
        def _():
            go_up[n].wait_recv()
            go_two[n].start()
            go_swapped[n].start()

        @pl.when(sends_up_two)
        def _():
            go_up_two[n].start()

    @pl.when(column == 1)
    def _():
        wait_recv(go_across)
        pass_on(go_one)

    @pl.when(has_down)
    def _():
        wait_recv(go_two)
        mine, other = distance(2)
        attend([(TWO, mine), (O_TWO, other)])

    @pl.when(has_far & (core == 1))
    def _():
        wait_recv(go_up_two)

    @pl.when(sends_across_far)
    def _():
        pass_on(go_across_far)

    @pl.when(has_far & (core == 1))
    def _():
        pass_on(far_to_sibling)

    @pl.when(has_down)
    def _():
        wait_recv(go_swapped)

    @pl.when(has_down & (column == 0))
    def _():
        pass_on(go_one)

    @pl.when(sends_up_one)
    def _():
        pass_on(go_up_one)

    @pl.when(has_down & (column == 1))
    def _():
        pass_on(go_three)

    gets_extra = has_far & (core == 0)
    mine, other = distance(1)

    @pl.when(has_one)
    def _():
        wait_recv(go_one)

    @pl.when(gets_extra)
    def _():
        wait_recv(far_to_sibling)
        attend([(ONE, mine), (O_ONE, other), (EXTRA, 7)])

    @pl.when(has_one & jnp.logical_not(gets_extra))
    def _():
        attend([(ONE, mine), (O_ONE, other)])

    @pl.when(has_far & (column == 0) & (core == 0))
    def _():
        wait_recv(go_up_one)

    @pl.when(has_far & (column == 0) & (core == 1))
    def _():
        wait_recv(go_across_far)

    @pl.when(has_far & (column == 0))
    def _():
        pass_on(go_three)

    @pl.when(has_three)
    def _():
        wait_recv(go_three)
        mine, other = distance(3)
        attend([(THREE, mine), (O_THREE, other)], last=True)

    @pl.when(jnp.logical_not(has_three))
    def _():
        for tile in range(TILES):
            finish(tile, acc_ref[tile])

    for when, flow in (
        (has_up, go_up),
        (column == 0, go_across),
        (has_down, go_swapped),
        (sends_up_two, go_up_two),
        (sends_across_far, go_across_far),
        (sends_up_one, go_up_one),
        (has_one, go_one),
        (has_down, go_two),
        (has_three, go_three),
        (core == 0, own_to_sibling),
        (has_far & (core == 1), far_to_sibling),
    ):

        @pl.when(when)
        def _(flow=flow):
            for copy in flow:
                copy.wait_send()


def on_device(z_count, queries, keys, values, spans):
    shape = jax.ShapeDtypeStruct(queries.shape, BF16)
    queries, keys, values = (
        pltpu.with_memory_space_constraint(array, pltpu.HBM) for array in (queries, keys, values)
    )
    return pl.pallas_call(
        functools.partial(kernel, z_count),
        out_shape=shape,
        in_specs=[pl.BlockSpec(memory_space=pltpu.HBM)] * 3 + [pl.BlockSpec(memory_space=pltpu.SMEM)],
        out_specs=pl.BlockSpec(memory_space=pltpu.VMEM),
        scratch_shapes=[
            pltpu.VMEM(queries.shape, BF16),
            pltpu.VMEM(keys.shape, BF16),
            pltpu.VMEM((9, HEAD, ROWS), BF16),
            pltpu.VMEM((9, ROWS, HEAD), BF16),
            pltpu.VMEM((TILES, TILE, 2 * HEAD), F32),
            pltpu.VMEM((TILES, TILE, HEAD), F32),
            pltpu.SemaphoreType.DMA((10, 2)),
            pltpu.SemaphoreType.DMA((10, 2)),
            pltpu.SemaphoreType.DMA((3,)),
        ],
        compiler_params=pltpu.CompilerParams(
            collective_id=1, has_side_effects=True, vmem_limit_bytes=52 * 2**20
        ),
    )(queries, keys, values, spans)


def solution(mesh):
    placed = (P("ctx", "tp"), P("ctx", "tp"), P("ctx", "tp"), P("ctx"))
    return jax.shard_map(
        functools.partial(on_device, mesh.shape["ctx"] // 4),
        mesh=mesh,
        in_specs=placed,
        out_specs=P("ctx", "tp"),
        check_vma=False,
    )
```
